32 devices in a mesh: ia: 8 (over z, y), ja: 2 (over core), ka: 2 (over x).
Axes of the slice: x: 2, y: 2, z: 4, core: 2. Of those that a mesh axis runs over, the one named last changes fastest.
Arguments:
- tensor: bfloat16 [64, 2048, 256], P('ia', 'ja', 'ka'), may hold values from -115200 to 115200
- factor_b: float32 [8, 2, 2, 64, 64], P('ia', 'ja', 'ka'), may hold values from -4.5 to 13.5
- factor_c: float32 [2, 8, 2, 8, 64], P('ka', 'ia', 'ja'), may hold values from -4.5 to 13.5
Outputs:
- factor_a: float32 [64, 64], P('ia')
- factor_b_out: float32 [8, 2, 2, 64, 64], P('ia', 'ja', 'ka')
The draws below stay inside these ranges and needn't reach their ends.
All inputs are finite; a program needn't handle non-finite values.
Results may differ from the reference program's by a relative error of at most 0.008.
Values may be sent and summed in bfloat16 or wider, within the bound.
A program may use at most 64 MiB of HBM per device.

```python
import jax
import jax.numpy as jnp
from jax import lax

R = 64
JB = 1024
KB = 128
I = 64
J = 2048
K = 256
JQ = 64
CQ = 8
N_IA = 8
N_JA = 2
N_KA = 2


def rising(position, total_count, top_value):
    return jnp.exp(jnp.log(top_value) * position / max(total_count - 1, 1))


def owner_grid():
    return jnp.arange(N_IA * N_JA * N_KA).reshape(N_IA, N_JA, N_KA).astype(jnp.float32)


def draw_tensor(key, part):
    top_value = 10.0
    scale_i = rising(jnp.arange(I).astype(jnp.float32), I, top_value)
    index_j = jnp.arange(J)
    block_j = index_j // JB
    inner_j = index_j % JB // JQ
    owner_j = inner_j // N_KA * (N_JA * N_KA) + block_j * N_KA + inner_j % N_KA
    scale_j = rising(owner_j.astype(jnp.float32), N_IA * N_JA * N_KA, 10.0)
    noise_field = jax.random.truncated_normal(key, -6.0, 6.0, (I, J, K), jnp.float32)
    return (noise_field * (64.0 * scale_i[:, None, None] * scale_j[None, :, None])).astype(jnp.bfloat16)


def draw_factor_b(key, part):
    top_value = 3.0
    owners = owner_grid()[:, :, :, None, None]
    values = jax.random.uniform(key, (N_IA, N_JA, N_KA, JQ, R), jnp.float32, -0.5, 1.5)
    return values * rising(owners, N_IA * N_JA * N_KA, top_value)


def draw_factor_c(key, part):
    top_value = 3.0
    owners = jnp.transpose(owner_grid(), (2, 0, 1))[:, :, :, None, None]
    values = jax.random.uniform(key, (N_KA, N_IA, N_JA, CQ, R), jnp.float32, -0.5, 1.5)
    return values * rising(owners, N_IA * N_JA * N_KA, top_value)


def setup_inputs(seed: int = 0) -> dict:
    streams_of = jax.random.split(jax.random.key(seed), 4)
    tensor = draw_tensor(jax.random.fold_in(streams_of[3], 71), 0)
    factor_b = draw_factor_b(jax.random.fold_in(streams_of[3], 71), 0)
    factor_c = draw_factor_c(jax.random.fold_in(streams_of[3], 71), 0)
    return dict(tensor=tensor, factor_b=factor_b, factor_c=factor_c)


epsilon = 1e-06

def solve_normal(gram_mat, rhs_rows):
    factor_low = jnp.linalg.cholesky(gram_mat)
    return jax.scipy.linalg.cho_solve((factor_low, True), rhs_rows.T).T

def reference(tensor, factor_b, factor_c):
    highest = lax.Precision.HIGHEST
    rows_b = jnp.transpose(factor_b, (1, 0, 2, 3, 4)).reshape(J, R)
    rows_c = factor_c.reshape(K, R)
    gram_b = jnp.dot(rows_b.T.astype(jnp.float32), rows_b.astype(jnp.float32), precision=highest, preferred_element_type=jnp.float32)
    gram_c = jnp.dot(rows_c.T.astype(jnp.float32), rows_c.astype(jnp.float32), precision=highest, preferred_element_type=jnp.float32)
    cast_c = rows_c.astype(jnp.bfloat16)
    cast_b = lax.optimization_barrier(rows_b.astype(jnp.bfloat16)).astype(jnp.float32)

    def first_pass(carry, block_index):
        slab_data = lax.dynamic_slice_in_dim(tensor, block_index * KB, KB, 2)
        c_part = lax.dynamic_slice_in_dim(cast_c, block_index * KB, KB, 0)
        block_y = jnp.dot(slab_data.reshape(I * J, KB).astype(jnp.float32), c_part.astype(jnp.float32), preferred_element_type=jnp.float32)
        block_y = block_y.astype(jnp.bfloat16).reshape(I, J, R)
        widened = lax.optimization_barrier(block_y).astype(jnp.float32)
        return (carry + jnp.einsum('ijr,jr->ir', widened, cast_b), block_y)
    block_ids = jnp.arange(N_KA, dtype=jnp.int32)
    mode_a, stored_y = lax.scan(first_pass, jnp.zeros((I, R), jnp.float32), block_ids)
    a_new = solve_normal(gram_b * gram_c, mode_a)
    factor_a = a_new * lax.rsqrt(lax.optimization_barrier(jnp.mean(a_new * a_new, axis=0)) + epsilon)
    gram_a = jnp.dot(factor_a.T.astype(jnp.float32), factor_a.astype(jnp.float32), precision=highest, preferred_element_type=jnp.float32)
    cast_a = lax.optimization_barrier(factor_a.astype(jnp.bfloat16)).astype(jnp.float32)

    def second_pass(carry, block_y):
        widened = block_y.astype(jnp.float32)
        return (carry + jnp.einsum('ijr,ir->jr', widened, cast_a), jnp.zeros((), jnp.float32))
    mode_b, unused = lax.scan(second_pass, jnp.zeros((J, R), jnp.float32), stored_y)
    b_new = solve_normal(gram_a * gram_c, mode_b)
    rows_out = b_new * lax.rsqrt(lax.optimization_barrier(jnp.mean(b_new * b_new, axis=0)) + epsilon)
    factor_b_out = jnp.transpose(rows_out.reshape(N_JA, N_IA, N_KA, JQ, R), (1, 0, 2, 3, 4))
    return (factor_a, factor_b_out)
```

```python
import functools

import jax
import jax.numpy as jnp
from jax import lax
from jax.experimental import pallas as pl
from jax.experimental.pallas import tpu as pltpu
from jax.sharding import PartitionSpec as P

epsilon = 1e-06
HIGHEST = lax.Precision.HIGHEST
MESH = pl.DeviceIdType.MESH
f32 = jnp.float32
bf16 = jnp.bfloat16


def solve_normal(gram_mat, rhs_rows):
    factor_low = jnp.linalg.cholesky(gram_mat)
    return jax.scipy.linalg.cho_solve((factor_low, True), rhs_rows.T).T


def self_gram(rows_data):
    return jnp.dot(rows_data.T, rows_data, precision=HIGHEST, preferred_element_type=f32)


def body(tensor, factor_b, factor_c):
    rank_cols = factor_b.shape[-1]
    own_b = factor_b.reshape(-1, rank_cols)
    own_c = factor_c.reshape(-1, rank_cols)
    rows_i, rows_j, rows_k = tensor.shape
    block_c = lax.all_gather(own_c.astype(bf16), ("ia", "ja"), axis=0, tiled=True)
    partial_value = jnp.einsum("ijk,kr->irj", tensor, block_c, preferred_element_type=f32).astype(bf16)
    block_b = lax.all_gather(own_b.astype(bf16), ("ia", "ka"), axis=0, tiled=True)
    mode_local = jnp.einsum("irj,jr->ir", partial_value, block_b, preferred_element_type=f32)
    mode_a = lax.psum(mode_local, ("ja", "ka"))
    gram_b, gram_c = lax.psum((self_gram(own_b), self_gram(own_c)), ("ia", "ja", "ka"))
    a_new = solve_normal(gram_b * gram_c, mode_a)
    count_i = rows_i * lax.axis_size("ia")
    squares = lax.psum(jnp.sum(a_new * a_new, axis=0), "ia")
    factor_a = a_new * lax.rsqrt(squares / count_i + epsilon)
    gram_a = lax.psum(self_gram(factor_a), "ia")
    cast_a = factor_a.astype(bf16)
    mode_b = lax.psum_scatter(
        jnp.einsum("irj,ir->jr", partial_value, cast_a, preferred_element_type=f32),
        ("ia", "ka"),
        scatter_dimension=0,
        tiled=True,
    )
    b_new = solve_normal(gram_a * gram_c, mode_b)
    sums_b = lax.psum(jnp.sum(b_new * b_new, axis=0), ("ia", "ja", "ka"))
    count_j = rows_j * lax.axis_size("ja")
    out_rows = b_new * lax.rsqrt(sums_b / count_j + epsilon)
    return (factor_a, out_rows.reshape(factor_b.shape))


def dot0(a, b):
    return lax.dot_general(a, b, (((0,), (0,)), ((), ())), precision=HIGHEST, preferred_element_type=f32)


def sweep_inverse(mat, rank):
    lane = lax.rem(lax.broadcasted_iota(jnp.int32, mat.shape, 1), rank)
    row_id = lax.broadcasted_iota(jnp.int32, mat.shape, 0)
    for k in range(rank):
        col = jnp.broadcast_to(mat[:, k : k + 1], mat.shape)
        inv = 1.0 / col[k : k + 1, :]
        row = mat[k : k + 1, :] * inv
        row_new = jnp.where(lane[k : k + 1, :] == k, -inv, row)
        new = jnp.where(lane == k, col * inv, mat - col * row)
        mat = jnp.where(row_id == k, row_new, new)
    return -mat


def kernel(
    dims, x_hbm, b_ref, c_ref, fa_out, fb_out,
    xv, yv, bbuf, cbuf, bq, gbs, gcs, mabuf, fas, mbs, mbr, sbuf,
    x_sem, send, recv,
):
    ni, nj, nk = dims
    pi, pj, pk = lax.axis_index("ia"), lax.axis_index("ja"), lax.axis_index("ka")
    n_b, n_c, n_all = ni * nk, ni * nj, ni * nj * nk
    slot_b, slot_c = pi * nk + pk, pi * nj + pj
    me = (pi * nj + pj) * nk + pk
    rows_i, rows_j, _ = xv.shape
    rank = b_ref.shape[-1]
    half = b_ref.shape[0] // 2
    rows_c = c_ref.shape[0]

    def dev_b(t):
        return (t // nk, pj, lax.rem(t, nk))

    def dev_c(t):
        return (t // nj, lax.rem(t, nj), pk)

    def dev_all(t):
        return (t // (nj * nk), lax.rem(t // nk, nj), lax.rem(t, nk))

    def copy_to(src, dst, s, dev):
        return pltpu.make_async_remote_copy(
            src_ref=src, dst_ref=dst, send_sem=send.at[s], recv_sem=recv.at[s], device_id=dev, device_id_type=MESH
        )

    def spread(buf, s, mine, n, dev):
        def step(d, carry):
            copy_to(buf.at[mine], buf.at[mine], s, dev(lax.rem(mine + d, n))).start()
            return carry

        lax.fori_loop(1, n, step, 0)

    def all_of(buf, s, n, dev):
        rest = buf.at[pl.ds(0, n - 1)]
        return copy_to(rest, rest, s, dev(0))

    load_x = pltpu.make_async_copy(x_hbm, xv, x_sem)
    load_x.start()

    barrier = pltpu.get_barrier_semaphore()

    def greet(d, carry):
        pl.semaphore_signal(barrier, inc=1, device_id=dev_all(lax.rem(me + d, n_all)), device_id_type=MESH)
        return carry

    lax.fori_loop(1, n_all, greet, 0)

    own_b = b_ref[...]
    own_c = c_ref[...]
    bbuf[slot_b] = jnp.concatenate([own_b[:half], own_b[half:]], axis=1)
    cbuf[slot_c] = jnp.concatenate([own_c, own_c], axis=1)

    pl.semaphore_wait(barrier, n_all - 1)

    spread(cbuf, 0, slot_c, n_c, dev_c)
    spread(bbuf, 1, slot_b, n_b, dev_b)

    all_of(cbuf, 0, n_c, dev_c).wait_recv()
    c_all = cbuf[...].reshape(n_c * rows_c, 2 * rank)
    low = lax.broadcasted_iota(jnp.int32, c_all.shape, 1) < rank
    zero = jnp.zeros_like(c_all)
    c_two = jnp.concatenate([jnp.where(low, c_all, zero), jnp.where(low, zero, c_all)], axis=0).astype(bf16)
    gcs[pk] = dot0(c_all, c_all)[:rank]

    def send_gc(d, carry):
        copy_to(gcs.at[pk], gcs.at[pk], 2, (pi, pj, lax.rem(pk + d, nk))).start()
        return carry

    lax.fori_loop(1, nk, send_gc, 0)
    load_x.wait()

    def make_y(i, carry):
        x = xv[i].reshape(n_b, 2 * half, xv.shape[2])
        left = x[:, :half].reshape(n_b * half, xv.shape[2])
        right = x[:, half:].reshape(n_b * half, xv.shape[2])
        y = jnp.dot(jnp.concatenate([left, right], axis=1), c_two, preferred_element_type=f32)
        yv[i] = y.astype(bf16)
        return carry

    lax.fori_loop(0, rows_i, make_y, 0)

    all_of(bbuf, 1, n_b, dev_b).wait_recv()
    b_all = bbuf[...].reshape(n_b * half, 2 * rank)
    gram = dot0(b_all, b_all)
    low = lax.broadcasted_iota(jnp.int32, (rank, 2 * rank), 1) < rank
    gram = jnp.where(low, gram[:rank], gram[rank:])
    gbs[pj] = gram + pltpu.roll(gram, rank, 1)

    def send_gb(d, carry):
        copy_to(gbs.at[pj], gbs.at[pj], 3, (pi, lax.rem(pj + d, nj), pk)).start()
        return carry

    lax.fori_loop(1, nj, send_gb, 0)
    bq[...] = b_all.astype(bf16).astype(f32)

    def make_ma(i, carry):
        mabuf[me, pl.ds(i, 1), :] = jnp.sum(yv[i].astype(f32) * bq[...], axis=0, keepdims=True)
        return carry

    lax.fori_loop(0, rows_i, make_ma, 0)
    spread(mabuf, 4, me, n_all, dev_all)

    all_of(gcs, 2, nk, dev_b).wait_recv()
    all_of(gbs, 3, nj, dev_b).wait_recv()
    gram_c = jnp.sum(gcs[...], axis=0)
    inv_a = sweep_inverse(jnp.sum(gbs[...], axis=0) * gram_c, rank)

    all_of(mabuf, 4, n_all, dev_all).wait_recv()
    mode_a = jnp.sum(mabuf[...].reshape(ni, nj * nk, rows_i, 2 * rank), axis=1).reshape(ni * rows_i, 2 * rank)
    a_new = jnp.dot(
        mode_a, jnp.concatenate([inv_a, inv_a], axis=0), precision=HIGHEST, preferred_element_type=f32
    )
    squares = jnp.sum(a_new * a_new, axis=0, keepdims=True)
    factor_a = a_new * lax.rsqrt(squares / (ni * rows_i) + epsilon)
    fas[...] = factor_a
    own_a = fas[pl.ds(pl.multiple_of(pi * rows_i, rows_i), rows_i), :]
    fa_out[...] = own_a[:, :rank]
    cast_a = own_a.astype(bf16).astype(f32)

    def make_mb(d, carry):
        t = lax.rem(slot_b + d, n_b)
        rows = pl.ds(pl.multiple_of(t * half, half), half)
        total = yv[0, rows, :].astype(f32) * cast_a[0:1]
        for i in range(1, rows_i):
            total += yv[i, rows, :].astype(f32) * cast_a[i : i + 1]
        mbs[t] = total

        copy_to(mbs.at[t], mbr.at[slot_b], 5, dev_b(t)).start()
        return carry

    lax.fori_loop(1, n_b, make_mb, 0)
    rows = pl.ds(pl.multiple_of(slot_b * half, half), half)
    total = yv[0, rows, :].astype(f32) * cast_a[0:1]
    for i in range(1, rows_i):
        total += yv[i, rows, :].astype(f32) * cast_a[i : i + 1]
    mbr[slot_b] = total

    gram_a = dot0(factor_a, factor_a)[:rank]
    inv_b = sweep_inverse(gram_a * gram_c, rank)
    zero = jnp.zeros_like(inv_b)
    inv_two = jnp.concatenate([jnp.where(low, inv_b, zero), jnp.where(low, zero, inv_b)], axis=0)

    all_of(mbr, 5, n_b, dev_b).wait_recv()
    mode_b = jnp.sum(mbr[...], axis=0)
    b_new = jnp.dot(mode_b, inv_two, precision=HIGHEST, preferred_element_type=f32)
    sbuf[me] = jnp.sum(b_new * b_new, axis=0, keepdims=True)
    spread(sbuf, 6, me, n_all, dev_all)

    all_of(cbuf, 0, n_c, dev_c).wait_send()
    all_of(bbuf, 1, n_b, dev_b).wait_send()
    all_of(gcs, 2, nk, dev_b).wait_send()
    all_of(gbs, 3, nj, dev_b).wait_send()
    all_of(mabuf, 4, n_all, dev_all).wait_send()
    all_of(mbr, 5, n_b, dev_b).wait_send()

    all_of(sbuf, 6, n_all, dev_all).wait_recv()
    sums = jnp.broadcast_to(jnp.sum(sbuf[...], axis=0), (8, 2 * rank))
    sums = (sums + pltpu.roll(sums, rank, 1))[0:1]
    out = b_new * lax.rsqrt(sums / (nj * rows_j) + epsilon)
    fb_out[0:half, :] = out[:, :rank]
    fb_out[half:, :] = out[:, rank:]
    all_of(sbuf, 6, n_all, dev_all).wait_send()


def fused(dims, tensor, factor_b, factor_c):
    ni, nj, nk = dims
    rank = factor_b.shape[-1]
    own_b = factor_b.reshape(-1, rank)
    own_c = factor_c.reshape(-1, rank)
    rows_i, rows_j, rows_k = tensor.shape
    half = own_b.shape[0] // 2
    n_b, n_c, n_all = ni * nk, ni * nj, ni * nj * nk
    wide = 2 * rank
    vmem = pl.BlockSpec(memory_space=pltpu.VMEM)
    fa, fb = pl.pallas_call(
        functools.partial(kernel, dims),
        out_shape=(
            jax.ShapeDtypeStruct((rows_i, rank), f32),
            jax.ShapeDtypeStruct(own_b.shape, f32),
        ),
        in_specs=[pl.BlockSpec(memory_space=pl.ANY), vmem, vmem],
        out_specs=(vmem, vmem),
        scratch_shapes=[
            pltpu.VMEM(tensor.shape, bf16),
            pltpu.VMEM((rows_i, n_b * half, wide), bf16),
            pltpu.VMEM((n_b, half, wide), f32),
            pltpu.VMEM((n_c, own_c.shape[0], wide), f32),
            pltpu.VMEM((n_b * half, wide), f32),
            pltpu.VMEM((nj, rank, wide), f32),
            pltpu.VMEM((nk, rank, wide), f32),
            pltpu.VMEM((n_all, rows_i, wide), f32),
            pltpu.VMEM((ni * rows_i, wide), f32),
            pltpu.VMEM((n_b, half, wide), f32),
            pltpu.VMEM((n_b, half, wide), f32),
            pltpu.VMEM((n_all, 1, wide), f32),
            pltpu.SemaphoreType.DMA,
            pltpu.SemaphoreType.DMA((7,)),
            pltpu.SemaphoreType.DMA((7,)),
        ],
        compiler_params=pltpu.CompilerParams(
            collective_id=0, has_side_effects=True, vmem_limit_bytes=63 * 1024 * 1024
        ),
    )(tensor, own_b, own_c)
    return fa, fb.reshape(factor_b.shape)


def solution(mesh):
    dims = tuple(mesh.shape[a] for a in ("ia", "ja", "ka"))

    def step(tensor, factor_b, factor_c):
        whole_tiles = (
            factor_b.shape[-2] % 32 == 0
            and factor_c.shape[-2] % 8 == 0
            and tensor.shape[0] % 8 == 0
            and factor_b.shape[-1] == 64
        )
        if whole_tiles:
            return fused(dims, tensor, factor_b, factor_c)
        return body(tensor, factor_b, factor_c)

    return jax.shard_map(
        step,
        mesh=mesh,
        in_specs=(
            P("ia", "ja", "ka"),
            P("ia", "ja", "ka", None, None),
            P("ka", "ia", "ja", None, None),
        ),
        out_specs=(P("ia", None), P("ia", "ja", "ka", None, None)),
        check_vma=False,
    )
```

```python
import functools

import jax
import jax.numpy as jnp
from jax import lax
from jax.experimental import pallas as pl
from jax.experimental.pallas import tpu as pltpu
from jax.sharding import PartitionSpec as P

epsilon = 1e-06
HIGHEST = lax.Precision.HIGHEST
MESH = pl.DeviceIdType.MESH
f32 = jnp.float32
bf16 = jnp.bfloat16


def solve_normal(gram_mat, rhs_rows):
    factor_low = jnp.linalg.cholesky(gram_mat)
    return jax.scipy.linalg.cho_solve((factor_low, True), rhs_rows.T).T


def self_gram(rows_data):
    return jnp.dot(rows_data.T, rows_data, precision=HIGHEST, preferred_element_type=f32)


def body(tensor, factor_b, factor_c):
    rank_cols = factor_b.shape[-1]
    own_b = factor_b.reshape(-1, rank_cols)
    own_c = factor_c.reshape(-1, rank_cols)
    rows_i, rows_j, rows_k = tensor.shape
    block_c = lax.all_gather(own_c.astype(bf16), ("ia", "ja"), axis=0, tiled=True)
    partial_value = jnp.einsum("ijk,kr->irj", tensor, block_c, preferred_element_type=f32).astype(bf16)
    block_b = lax.all_gather(own_b.astype(bf16), ("ia", "ka"), axis=0, tiled=True)
    mode_local = jnp.einsum("irj,jr->ir", partial_value, block_b, preferred_element_type=f32)
    mode_a = lax.psum(mode_local, ("ja", "ka"))
    gram_b, gram_c = lax.psum((self_gram(own_b), self_gram(own_c)), ("ia", "ja", "ka"))
    a_new = solve_normal(gram_b * gram_c, mode_a)
    count_i = rows_i * lax.axis_size("ia")
    squares = lax.psum(jnp.sum(a_new * a_new, axis=0), "ia")
    factor_a = a_new * lax.rsqrt(squares / count_i + epsilon)
    gram_a = lax.psum(self_gram(factor_a), "ia")
    cast_a = factor_a.astype(bf16)
    mode_b = lax.psum_scatter(
        jnp.einsum("irj,ir->jr", partial_value, cast_a, preferred_element_type=f32),
        ("ia", "ka"),
        scatter_dimension=0,
        tiled=True,
    )
    b_new = solve_normal(gram_a * gram_c, mode_b)
    sums_b = lax.psum(jnp.sum(b_new * b_new, axis=0), ("ia", "ja", "ka"))
    count_j = rows_j * lax.axis_size("ja")
    out_rows = b_new * lax.rsqrt(sums_b / count_j + epsilon)
    return (factor_a, out_rows.reshape(factor_b.shape))


def dot0(a, b):
    return lax.dot_general(a, b, (((0,), (0,)), ((), ())), precision=HIGHEST, preferred_element_type=f32)


def sweep_inverse(mat, rank):
    lane = lax.rem(lax.broadcasted_iota(jnp.int32, mat.shape, 1), rank)
    row_id = lax.broadcasted_iota(jnp.int32, mat.shape, 0)
    for k in range(rank):
        col = jnp.broadcast_to(mat[:, k : k + 1], mat.shape)
        inv = 1.0 / col[k : k + 1, :]
        row = mat[k : k + 1, :] * inv
        row_new = jnp.where(lane[k : k + 1, :] == k, -inv, row)
        new = jnp.where(lane == k, col * inv, mat - col * row)
        mat = jnp.where(row_id == k, row_new, new)
    return -mat


def kernel(
    dims, x_hbm, b_ref, c_ref, fa_out, fb_out,
    xv, yv, bhi, blo, cbuf, bq, gbs, gcs, mas, mabuf, fas, mbs, mbr, sbuf,
    x_sem, send, recv,
):
    ni, nj, nk = dims
    pi, pj, pk = lax.axis_index("ia"), lax.axis_index("ja"), lax.axis_index("ka")
    n_b, n_c, n_all = ni * nk, ni * nj, ni * nj * nk
    slot_b, slot_c = pi * nk + pk, pi * nj + pj
    me = (pi * nj + pj) * nk + pk
    rows_i, rows_j, _ = xv.shape
    rank = b_ref.shape[-1]
    half = b_ref.shape[0] // 2
    rows_c = c_ref.shape[0]

    def dev_b(t):
        return (t // nk, pj, lax.rem(t, nk))

    def dev_c(t):
        return (t // nj, lax.rem(t, nj), pk)

    def dev_all(t):
        return (t // (nj * nk), lax.rem(t // nk, nj), lax.rem(t, nk))

    def copy_to(src, dst, s, dev):
        return pltpu.make_async_remote_copy(
            src_ref=src, dst_ref=dst, send_sem=send.at[s], recv_sem=recv.at[s], device_id=dev, device_id_type=MESH
        )

    def spread(buf, s, mine, n, dev):
        def step(d, carry):
            copy_to(buf.at[mine], buf.at[mine], s, dev(lax.rem(mine + d, n))).start()
            return carry

        lax.fori_loop(1, n, step, 0)

    def all_of(buf, s, n, dev):
        rest = buf.at[pl.ds(0, n - 1)]
        return copy_to(rest, rest, s, dev(0))

    load_x = pltpu.make_async_copy(x_hbm, xv, x_sem)
    load_x.start()

    barrier = pltpu.get_barrier_semaphore()

    def greet(d, carry):
        pl.semaphore_signal(barrier, inc=1, device_id=dev_all(lax.rem(me + d, n_all)), device_id_type=MESH)
        return carry

    lax.fori_loop(1, n_all, greet, 0)

    own_b = b_ref[...]
    own_c = c_ref[...]
    wide_b = jnp.concatenate([own_b[:half], own_b[half:]], axis=1)
    high_b = wide_b.astype(bf16)
    bhi[slot_b] = high_b
    blo[slot_b] = (wide_b - high_b.astype(f32)).astype(bf16)
    cbuf[slot_c] = jnp.concatenate([own_c, own_c], axis=1)

    pl.semaphore_wait(barrier, n_all - 1)

    spread(cbuf, 0, slot_c, n_c, dev_c)
    spread(bhi, 1, slot_b, n_b, dev_b)
    spread(blo, 7, slot_b, n_b, dev_b)

    all_of(cbuf, 0, n_c, dev_c).wait_recv()
    c_all = cbuf[...].reshape(n_c * rows_c, 2 * rank)
    low = lax.broadcasted_iota(jnp.int32, c_all.shape, 1) < rank
    zero = jnp.zeros_like(c_all)
    c_two = jnp.concatenate([jnp.where(low, c_all, zero), jnp.where(low, zero, c_all)], axis=0).astype(bf16)
    gcs[pk] = dot0(c_all, c_all)[:rank]

    def send_gc(d, carry):
        copy_to(gcs.at[pk], gcs.at[pk], 2, (pi, pj, lax.rem(pk + d, nk))).start()
        return carry

    lax.fori_loop(1, nk, send_gc, 0)
    load_x.wait()

    def make_y(i, carry):
        x = xv[i].reshape(n_b, 2 * half, xv.shape[2])
        left = x[:, :half].reshape(n_b * half, xv.shape[2])
        right = x[:, half:].reshape(n_b * half, xv.shape[2])
        y = jnp.dot(jnp.concatenate([left, right], axis=1), c_two, preferred_element_type=f32)
        yv[i] = y.astype(bf16)
        return carry

    lax.fori_loop(0, rows_i, make_y, 0)

    all_of(bhi, 1, n_b, dev_b).wait_recv()
    bq[...] = bhi[...].reshape(n_b * half, 2 * rank).astype(f32)

    def make_ma(i, carry):
        mas[pl.ds(i, 1), :] = jnp.sum(yv[i].astype(f32) * bq[...], axis=0, keepdims=True)
        return carry

    lax.fori_loop(0, rows_i, make_ma, 0)
    part = mas[...] + pltpu.roll(mas[...], rank, 1)
    low = lax.broadcasted_iota(jnp.int32, (rows_i // 2, 2 * rank), 1) < rank
    mabuf[me] = jnp.where(low, part[: rows_i // 2], part[rows_i // 2 :])
    spread(mabuf, 4, me, n_all, dev_all)

    all_of(blo, 7, n_b, dev_b).wait_recv()
    b_all = bq[...] + blo[...].reshape(n_b * half, 2 * rank).astype(f32)
    gram = dot0(b_all, b_all)
    low = lax.broadcasted_iota(jnp.int32, (rank, 2 * rank), 1) < rank
    gram = jnp.where(low, gram[:rank], gram[rank:])
    gbs[pj] = gram + pltpu.roll(gram, rank, 1)

    def send_gb(d, carry):
        copy_to(gbs.at[pj], gbs.at[pj], 3, (pi, lax.rem(pj + d, nj), pk)).start()
        return carry

    lax.fori_loop(1, nj, send_gb, 0)

    all_of(gcs, 2, nk, dev_b).wait_recv()
    all_of(gbs, 3, nj, dev_b).wait_recv()
    gram_c = jnp.sum(gcs[...], axis=0)
    inv_a = sweep_inverse(jnp.sum(gbs[...], axis=0) * gram_c, rank)

    all_of(mabuf, 4, n_all, dev_all).wait_recv()
    mode_a = jnp.sum(mabuf[...].reshape(ni, nj * nk, rows_i // 2, 2 * rank), axis=1)
    first = lax.broadcasted_iota(jnp.int32, mode_a.shape, 2) < rank
    zero = jnp.zeros_like(mode_a)
    mode_a = jnp.concatenate([jnp.where(first, mode_a, zero), jnp.where(first, zero, mode_a)], axis=1)
    mode_a = mode_a.reshape(ni * rows_i, 2 * rank)
    a_new = jnp.dot(
        mode_a, jnp.concatenate([inv_a, inv_a], axis=0), precision=HIGHEST, preferred_element_type=f32
    )
    squares = jnp.sum(a_new * a_new, axis=0, keepdims=True)
    factor_a = a_new * lax.rsqrt(squares / (ni * rows_i) + epsilon)
    fas[...] = factor_a
    own_a = fas[pl.ds(pl.multiple_of(pi * rows_i, rows_i), rows_i), :]
    fa_out[...] = own_a[:, :rank]
    cast_a = own_a.astype(bf16).astype(f32)

    def make_mb(d, carry):
        t = lax.rem(slot_b + d, n_b)
        rows = pl.ds(pl.multiple_of(t * half, half), half)
        total = yv[0, rows, :].astype(f32) * cast_a[0:1]
        for i in range(1, rows_i):
            total += yv[i, rows, :].astype(f32) * cast_a[i : i + 1]
        mbs[t] = total.astype(bf16)

        copy_to(mbs.at[t], mbr.at[slot_b], 5, dev_b(t)).start()
        return carry

    lax.fori_loop(1, n_b, make_mb, 0)
    rows = pl.ds(pl.multiple_of(slot_b * half, half), half)
    total = yv[0, rows, :].astype(f32) * cast_a[0:1]
    for i in range(1, rows_i):
        total += yv[i, rows, :].astype(f32) * cast_a[i : i + 1]
    mbr[slot_b] = total.astype(bf16)

    gram_a = dot0(factor_a, factor_a)[:rank]
    inv_b = sweep_inverse(gram_a * gram_c, rank)
    zero = jnp.zeros_like(inv_b)
    inv_two = jnp.concatenate([jnp.where(low, inv_b, zero), jnp.where(low, zero, inv_b)], axis=0)

    all_of(mbr, 5, n_b, dev_b).wait_recv()
    mode_b = jnp.sum(mbr[...].astype(f32), axis=0)
    b_new = jnp.dot(mode_b, inv_two, precision=HIGHEST, preferred_element_type=f32)
    sbuf[me] = jnp.sum(b_new * b_new, axis=0, keepdims=True)
    spread(sbuf, 6, me, n_all, dev_all)

    all_of(cbuf, 0, n_c, dev_c).wait_send()
    all_of(bhi, 1, n_b, dev_b).wait_send()
    all_of(blo, 7, n_b, dev_b).wait_send()
    all_of(gcs, 2, nk, dev_b).wait_send()
    all_of(gbs, 3, nj, dev_b).wait_send()
    all_of(mabuf, 4, n_all, dev_all).wait_send()
    all_of(mbr, 5, n_b, dev_b).wait_send()

    all_of(sbuf, 6, n_all, dev_all).wait_recv()
    sums = jnp.broadcast_to(jnp.sum(sbuf[...], axis=0), (8, 2 * rank))
    sums = (sums + pltpu.roll(sums, rank, 1))[0:1]
    out = b_new * lax.rsqrt(sums / (nj * rows_j) + epsilon)
    fb_out[0:half, :] = out[:, :rank]
    fb_out[half:, :] = out[:, rank:]
    all_of(sbuf, 6, n_all, dev_all).wait_send()


def place(a_ref, b_ref, a_out, b_out, sem):
    first = pltpu.make_async_copy(a_ref, a_out, sem.at[0])
    second = pltpu.make_async_copy(b_ref, b_out, sem.at[1])
    second.start()
    first.start()
    second.wait()
    first.wait()


def fused(dims, tensor, factor_b, factor_c):
    ni, nj, nk = dims
    rank = factor_b.shape[-1]
    own_b = factor_b.reshape(-1, rank)
    own_c = factor_c.reshape(-1, rank)
    rows_i, rows_j, rows_k = tensor.shape
    half = own_b.shape[0] // 2
    n_b, n_c, n_all = ni * nk, ni * nj, ni * nj * nk
    wide = 2 * rank
    vmem = pl.BlockSpec(memory_space=pltpu.VMEM)
    fa, fb = pl.pallas_call(
        functools.partial(kernel, dims),
        out_shape=(
            jax.ShapeDtypeStruct((rows_i, rank), f32),
            jax.ShapeDtypeStruct(own_b.shape, f32),
        ),
        in_specs=[pl.BlockSpec(memory_space=pl.ANY), vmem, vmem],
        out_specs=(vmem, vmem),
        scratch_shapes=[
            pltpu.VMEM(tensor.shape, bf16),
            pltpu.VMEM((rows_i, n_b * half, wide), bf16),
            pltpu.VMEM((n_b, half, wide), bf16),
            pltpu.VMEM((n_b, half, wide), bf16),
            pltpu.VMEM((n_c, own_c.shape[0], wide), f32),
            pltpu.VMEM((n_b * half, wide), f32),
            pltpu.VMEM((nj, rank, wide), f32),
            pltpu.VMEM((nk, rank, wide), f32),
            pltpu.VMEM((rows_i, wide), f32),
            pltpu.VMEM((n_all, rows_i // 2, wide), f32),
            pltpu.VMEM((ni * rows_i, wide), f32),
            pltpu.VMEM((n_b, half, wide), bf16),
            pltpu.VMEM((n_b, half, wide), bf16),
            pltpu.VMEM((n_all, 1, wide), f32),
            pltpu.SemaphoreType.DMA,
            pltpu.SemaphoreType.DMA((8,)),
            pltpu.SemaphoreType.DMA((8,)),
        ],
        compiler_params=pltpu.CompilerParams(
            collective_id=0, has_side_effects=True, vmem_limit_bytes=63 * 1024 * 1024
        ),
    )(tensor, own_b, own_c)
    fa, fb = pl.pallas_call(
        place,
        out_shape=(jax.ShapeDtypeStruct(fa.shape, f32), jax.ShapeDtypeStruct(fb.shape, f32)),
        in_specs=[vmem, vmem],
        out_specs=(pl.BlockSpec(memory_space=pl.ANY), pl.BlockSpec(memory_space=pl.ANY)),
        scratch_shapes=[pltpu.SemaphoreType.DMA((2,))],
    )(fa, fb)
    return fa, fb.reshape(factor_b.shape)


def solution(mesh):
    dims = tuple(mesh.shape[a] for a in ("ia", "ja", "ka"))

    def step(tensor, factor_b, factor_c):
        whole_tiles = (
            factor_b.shape[-2] % 32 == 0
            and factor_c.shape[-2] % 8 == 0
            and tensor.shape[0] % 8 == 0
            and factor_b.shape[-1] == 64
        )
        if whole_tiles:
            return fused(dims, tensor, factor_b, factor_c)
        return body(tensor, factor_b, factor_c)

    return jax.shard_map(
        step,
        mesh=mesh,
        in_specs=(
            P("ia", "ja", "ka"),
            P("ia", "ja", "ka", None, None),
            P("ka", "ia", "ja", None, None),
        ),
        out_specs=(P("ia", None), P("ia", "ja", "ka", None, None)),
        check_vma=False,
    )
```

```python
import functools

import jax
import jax.numpy as jnp
from jax import lax
from jax.experimental import pallas as pl
from jax.experimental.pallas import tpu as pltpu
from jax.sharding import PartitionSpec as P

epsilon = 1e-06
HIGHEST = lax.Precision.HIGHEST
MESH = pl.DeviceIdType.MESH
f32 = jnp.float32
bf16 = jnp.bfloat16


def solve_normal(gram_mat, rhs_rows):
    factor_low = jnp.linalg.cholesky(gram_mat)
    return jax.scipy.linalg.cho_solve((factor_low, True), rhs_rows.T).T


def self_gram(rows_data):
    return jnp.dot(rows_data.T, rows_data, precision=HIGHEST, preferred_element_type=f32)


def body(tensor, factor_b, factor_c):
    rank_cols = factor_b.shape[-1]
    own_b = factor_b.reshape(-1, rank_cols)
    own_c = factor_c.reshape(-1, rank_cols)
    rows_i, rows_j, rows_k = tensor.shape
    block_c = lax.all_gather(own_c.astype(bf16), ("ia", "ja"), axis=0, tiled=True)
    partial_value = jnp.einsum("ijk,kr->irj", tensor, block_c, preferred_element_type=f32).astype(bf16)
    block_b = lax.all_gather(own_b.astype(bf16), ("ia", "ka"), axis=0, tiled=True)
    mode_local = jnp.einsum("irj,jr->ir", partial_value, block_b, preferred_element_type=f32)
    mode_a = lax.psum(mode_local, ("ja", "ka"))
    gram_b, gram_c = lax.psum((self_gram(own_b), self_gram(own_c)), ("ia", "ja", "ka"))
    a_new = solve_normal(gram_b * gram_c, mode_a)
    count_i = rows_i * lax.axis_size("ia")
    squares = lax.psum(jnp.sum(a_new * a_new, axis=0), "ia")
    factor_a = a_new * lax.rsqrt(squares / count_i + epsilon)
    gram_a = lax.psum(self_gram(factor_a), "ia")
    cast_a = factor_a.astype(bf16)
    mode_b = lax.psum_scatter(
        jnp.einsum("irj,ir->jr", partial_value, cast_a, preferred_element_type=f32),
        ("ia", "ka"),
        scatter_dimension=0,
        tiled=True,
    )
    b_new = solve_normal(gram_a * gram_c, mode_b)
    sums_b = lax.psum(jnp.sum(b_new * b_new, axis=0), ("ia", "ja", "ka"))
    count_j = rows_j * lax.axis_size("ja")
    out_rows = b_new * lax.rsqrt(sums_b / count_j + epsilon)
    return (factor_a, out_rows.reshape(factor_b.shape))


def dot0(a, b):
    return lax.dot_general(a, b, (((0,), (0,)), ((), ())), precision=HIGHEST, preferred_element_type=f32)


def sweep_inverse(mat, rank):
    lane = lax.rem(lax.broadcasted_iota(jnp.int32, mat.shape, 1), rank)
    row_id = lax.broadcasted_iota(jnp.int32, mat.shape, 0)
    diag = jnp.where(lane == row_id, mat, 0.0)
    scale = lax.rsqrt(jnp.sum(diag, axis=0, keepdims=True))
    scale = lax.rsqrt(jnp.sum(diag[:, :rank], axis=1, keepdims=True)) * scale
    mat = mat * scale
    for k in range(0, rank, 2):
        col1 = jnp.broadcast_to(mat[:, k : k + 1], mat.shape)
        col2 = jnp.broadcast_to(mat[:, k + 1 : k + 2], mat.shape)
        row1, row2 = mat[k : k + 1, :], mat[k + 1 : k + 2, :]
        p11, p12, p22 = col1[k : k + 1, :], col2[k : k + 1, :], col2[k + 1 : k + 2, :]
        inv = 1.0 / (p11 * p22 - p12 * p12)
        q11, q12, q22 = p22 * inv, -p12 * inv, p11 * inv
        new1 = q11 * row1 + q12 * row2
        new2 = q12 * row1 + q22 * row2
        new = mat - col1 * new1 - col2 * new2
        new = jnp.where(lane == k, q11 * col1 + q12 * col2, new)
        new = jnp.where(lane == k + 1, q12 * col1 + q22 * col2, new)
        lane1 = lane[0:1, :]
        new1 = jnp.where(lane1 == k, -q11, jnp.where(lane1 == k + 1, -q12, new1))
        new2 = jnp.where(lane1 == k, -q12, jnp.where(lane1 == k + 1, -q22, new2))
        mat = jnp.where(row_id == k, new1, jnp.where(row_id == k + 1, new2, new))
    return -mat * scale


def kernel(
    dims, x_hbm, b_ref, c_ref, fa_out, fb_out,
    xv, yv, bhi, blo, cbuf, bq, gbs, gcs, mas, mabuf, fas, mbs, mbr, sbuf,
    x_sem, send, recv,
):
    ni, nj, nk = dims
    pi, pj, pk = lax.axis_index("ia"), lax.axis_index("ja"), lax.axis_index("ka")
    n_b, n_c, n_all = ni * nk, ni * nj, ni * nj * nk
    slot_b, slot_c = pi * nk + pk, pi * nj + pj
    me = (pi * nj + pj) * nk + pk
    rows_i, rows_j, _ = xv.shape
    rank = b_ref.shape[-1]
    half = b_ref.shape[0] // 2
    rows_c = c_ref.shape[0]

    def dev_b(t):
        return (t // nk, pj, lax.rem(t, nk))

    def dev_c(t):
        return (t // nj, lax.rem(t, nj), pk)

    def dev_all(t):
        return (t // (nj * nk), lax.rem(t // nk, nj), lax.rem(t, nk))

    def copy_to(src, dst, s, dev):
        return pltpu.make_async_remote_copy(
            src_ref=src, dst_ref=dst, send_sem=send.at[s], recv_sem=recv.at[s], device_id=dev, device_id_type=MESH
        )

    def spread(buf, s, mine, n, dev):
        def step(d, carry):
            copy_to(buf.at[mine], buf.at[mine], s, dev(lax.rem(mine + d, n))).start()
            return carry

        lax.fori_loop(1, n, step, 0)

    def all_of(buf, s, n, dev):
        rest = buf.at[pl.ds(0, n - 1)]
        return copy_to(rest, rest, s, dev(0))

    load_x = pltpu.make_async_copy(x_hbm, xv, x_sem)
    load_x.start()

    barrier = pltpu.get_barrier_semaphore()

    def greet(d, carry):
        pl.semaphore_signal(barrier, inc=1, device_id=dev_all(lax.rem(me + d, n_all)), device_id_type=MESH)
        return carry

    lax.fori_loop(1, n_all, greet, 0)

    own_b = b_ref[...]
    own_c = c_ref[...]
    wide_b = jnp.concatenate([own_b[:half], own_b[half:]], axis=1)
    high_b = wide_b.astype(bf16)
    bhi[slot_b] = high_b
    blo[slot_b] = (wide_b - high_b.astype(f32)).astype(bf16)
    cbuf[slot_c] = jnp.concatenate([own_c[: rows_c // 2], own_c[rows_c // 2 :]], axis=1)

    pl.semaphore_wait(barrier, n_all - 1)

    spread(cbuf, 0, slot_c, n_c, dev_c)
    spread(bhi, 1, slot_b, n_b, dev_b)
    spread(blo, 7, slot_b, n_b, dev_b)

    all_of(cbuf, 0, n_c, dev_c).wait_recv()
    c_all = cbuf[...]
    first = lax.broadcasted_iota(jnp.int32, c_all.shape, 2) < rank
    zero = jnp.zeros_like(c_all)
    c_odd = jnp.where(first, zero, c_all).reshape(n_c * rows_c // 2, 2 * rank)
    c_odd = pltpu.roll(c_odd, rank, 1).reshape(c_all.shape)
    c_left = jnp.concatenate([jnp.where(first, c_all, zero), c_odd], axis=1).reshape(n_c * rows_c, 2 * rank)
    c_right = pltpu.roll(c_left, rank, 1)
    c_two = jnp.concatenate([c_left, c_right], axis=0).astype(bf16)
    c_all = c_left + c_right
    gcs[pk] = dot0(c_all, c_all)[:rank]

    def send_gc(d, carry):
        copy_to(gcs.at[pk], gcs.at[pk], 2, (pi, pj, lax.rem(pk + d, nk))).start()
        return carry

    lax.fori_loop(1, nk, send_gc, 0)
    load_x.wait()

    def make_y(i, carry):
        x = xv[i].reshape(n_b, 2 * half, xv.shape[2])
        left = x[:, :half].reshape(n_b * half, xv.shape[2])
        right = x[:, half:].reshape(n_b * half, xv.shape[2])
        y = jnp.dot(jnp.concatenate([left, right], axis=1), c_two, preferred_element_type=f32)
        yv[i] = y.astype(bf16)
        return carry

    lax.fori_loop(0, rows_i, make_y, 0)

    all_of(bhi, 1, n_b, dev_b).wait_recv()
    bq[...] = bhi[...].reshape(n_b * half, 2 * rank).astype(f32)

    def make_ma(i, carry):
        mas[pl.ds(i, 1), :] = jnp.sum(yv[i].astype(f32) * bq[...], axis=0, keepdims=True)
        return carry

    lax.fori_loop(0, rows_i, make_ma, 0)
    part = mas[...] + pltpu.roll(mas[...], rank, 1)
    low = lax.broadcasted_iota(jnp.int32, (rows_i // 2, 2 * rank), 1) < rank
    mabuf[me] = jnp.where(low, part[: rows_i // 2], part[rows_i // 2 :])
    spread(mabuf, 4, me, n_all, dev_all)

    all_of(blo, 7, n_b, dev_b).wait_recv()
    b_all = bq[...] + blo[...].reshape(n_b * half, 2 * rank).astype(f32)
    gram = dot0(b_all, b_all)
    low = lax.broadcasted_iota(jnp.int32, (rank, 2 * rank), 1) < rank
    gram = jnp.where(low, gram[:rank], gram[rank:])
    gbs[pj] = gram + pltpu.roll(gram, rank, 1)

    def send_gb(d, carry):
        copy_to(gbs.at[pj], gbs.at[pj], 3, (pi, lax.rem(pj + d, nj), pk)).start()
        return carry

    lax.fori_loop(1, nj, send_gb, 0)

    all_of(gcs, 2, nk, dev_b).wait_recv()
    all_of(gbs, 3, nj, dev_b).wait_recv()
    gram_c = jnp.sum(gcs[...], axis=0)
    inv_a = sweep_inverse(jnp.sum(gbs[...], axis=0) * gram_c, rank)

    all_of(mabuf, 4, n_all, dev_all).wait_recv()
    mode_a = jnp.sum(mabuf[...].reshape(ni, nj * nk, rows_i // 2, 2 * rank), axis=1)
    first = lax.broadcasted_iota(jnp.int32, mode_a.shape, 2) < rank
    zero = jnp.zeros_like(mode_a)
    mode_a = jnp.concatenate([jnp.where(first, mode_a, zero), jnp.where(first, zero, mode_a)], axis=1)
    mode_a = mode_a.reshape(ni * rows_i, 2 * rank)
    a_new = jnp.dot(
        mode_a, jnp.concatenate([inv_a, inv_a], axis=0), precision=HIGHEST, preferred_element_type=f32
    )
    squares = jnp.sum(a_new * a_new, axis=0, keepdims=True)
    factor_a = a_new * lax.rsqrt(squares / (ni * rows_i) + epsilon)
    fas[...] = factor_a
    own_a = fas[pl.ds(pl.multiple_of(pi * rows_i, rows_i), rows_i), :]
    fa_out[...] = own_a[:, :rank]
    cast_a = own_a.astype(bf16).astype(f32)

    def make_mb(d, carry):
        t = lax.rem(slot_b + d, n_b)
        rows = pl.ds(pl.multiple_of(t * half, half), half)
        total = yv[0, rows, :].astype(f32) * cast_a[0:1]
        for i in range(1, rows_i):
            total += yv[i, rows, :].astype(f32) * cast_a[i : i + 1]
        mbs[t] = total.astype(bf16)

        copy_to(mbs.at[t], mbr.at[slot_b], 5, dev_b(t)).start()
        return carry

    lax.fori_loop(1, n_b, make_mb, 0)
    rows = pl.ds(pl.multiple_of(slot_b * half, half), half)
    total = yv[0, rows, :].astype(f32) * cast_a[0:1]
    for i in range(1, rows_i):
        total += yv[i, rows, :].astype(f32) * cast_a[i : i + 1]
    mbr[slot_b] = total.astype(bf16)

    gram_a = dot0(factor_a, factor_a)[:rank]
    inv_b = sweep_inverse(gram_a * gram_c, rank)
    zero = jnp.zeros_like(inv_b)
    inv_two = jnp.concatenate([jnp.where(low, inv_b, zero), jnp.where(low, zero, inv_b)], axis=0)

    all_of(mbr, 5, n_b, dev_b).wait_recv()
    mode_b = jnp.sum(mbr[...].astype(f32), axis=0)
    b_new = jnp.dot(mode_b, inv_two, precision=HIGHEST, preferred_element_type=f32)
    sbuf[me] = jnp.sum(b_new * b_new, axis=0, keepdims=True)
    spread(sbuf, 6, me, n_all, dev_all)

    all_of(cbuf, 0, n_c, dev_c).wait_send()
    all_of(bhi, 1, n_b, dev_b).wait_send()
    all_of(blo, 7, n_b, dev_b).wait_send()
    all_of(gcs, 2, nk, dev_b).wait_send()
    all_of(gbs, 3, nj, dev_b).wait_send()
    all_of(mabuf, 4, n_all, dev_all).wait_send()
    all_of(mbr, 5, n_b, dev_b).wait_send()

    all_of(sbuf, 6, n_all, dev_all).wait_recv()
    sums = jnp.broadcast_to(jnp.sum(sbuf[...], axis=0), (8, 2 * rank))
    sums = (sums + pltpu.roll(sums, rank, 1))[0:1]
    out = b_new * lax.rsqrt(sums / (nj * rows_j) + epsilon)
    fb_out[0:half, :] = out[:, :rank]
    fb_out[half:, :] = out[:, rank:]
    all_of(sbuf, 6, n_all, dev_all).wait_send()


def place(a_ref, b_ref, a_out, b_out, sem):
    first = pltpu.make_async_copy(a_ref, a_out, sem.at[0])
    second = pltpu.make_async_copy(b_ref, b_out, sem.at[1])
    second.start()
    first.start()
    second.wait()
    first.wait()


def fused(dims, tensor, factor_b, factor_c):
    ni, nj, nk = dims
    rank = factor_b.shape[-1]
    own_b = factor_b.reshape(-1, rank)
    own_c = factor_c.reshape(-1, rank)
    rows_i, rows_j, rows_k = tensor.shape
    half = own_b.shape[0] // 2
    n_b, n_c, n_all = ni * nk, ni * nj, ni * nj * nk
    wide = 2 * rank
    vmem = pl.BlockSpec(memory_space=pltpu.VMEM)
    fa, fb = pl.pallas_call(
        functools.partial(kernel, dims),
        out_shape=(
            jax.ShapeDtypeStruct((rows_i, rank), f32),
            jax.ShapeDtypeStruct(own_b.shape, f32),
        ),
        in_specs=[pl.BlockSpec(memory_space=pl.ANY), vmem, vmem],
        out_specs=(vmem, vmem),
        scratch_shapes=[
            pltpu.VMEM(tensor.shape, bf16),
            pltpu.VMEM((rows_i, n_b * half, wide), bf16),
            pltpu.VMEM((n_b, half, wide), bf16),
            pltpu.VMEM((n_b, half, wide), bf16),
            pltpu.VMEM((n_c, own_c.shape[0] // 2, wide), f32),
            pltpu.VMEM((n_b * half, wide), f32),
            pltpu.VMEM((nj, rank, wide), f32),
            pltpu.VMEM((nk, rank, wide), f32),
            pltpu.VMEM((rows_i, wide), f32),
            pltpu.VMEM((n_all, rows_i // 2, wide), f32),
            pltpu.VMEM((ni * rows_i, wide), f32),
            pltpu.VMEM((n_b, half, wide), bf16),
            pltpu.VMEM((n_b, half, wide), bf16),
            pltpu.VMEM((n_all, 1, wide), f32),
            pltpu.SemaphoreType.DMA,
            pltpu.SemaphoreType.DMA((8,)),
            pltpu.SemaphoreType.DMA((8,)),
        ],
        compiler_params=pltpu.CompilerParams(
            collective_id=0, has_side_effects=True, vmem_limit_bytes=63 * 1024 * 1024
        ),
    )(tensor, own_b, own_c)
    fa, fb = pl.pallas_call(
        place,
        out_shape=(jax.ShapeDtypeStruct(fa.shape, f32), jax.ShapeDtypeStruct(fb.shape, f32)),
        in_specs=[vmem, vmem],
        out_specs=(pl.BlockSpec(memory_space=pl.ANY), pl.BlockSpec(memory_space=pl.ANY)),
        scratch_shapes=[pltpu.SemaphoreType.DMA((2,))],
    )(fa, fb)
    return fa, fb.reshape(factor_b.shape)


def solution(mesh):
    dims = tuple(mesh.shape[a] for a in ("ia", "ja", "ka"))

    def step(tensor, factor_b, factor_c):
        whole_tiles = (
            factor_b.shape[-2] % 32 == 0
            and factor_c.shape[-2] % 8 == 0
            and tensor.shape[0] % 8 == 0
            and factor_b.shape[-1] == 64
        )
        if whole_tiles:
            return fused(dims, tensor, factor_b, factor_c)
        return body(tensor, factor_b, factor_c)

    return jax.shard_map(
        step,
        mesh=mesh,
        in_specs=(
            P("ia", "ja", "ka"),
            P("ia", "ja", "ka", None, None),
            P("ka", "ia", "ja", None, None),
        ),
        out_specs=(P("ia", None), P("ia", "ja", "ka", None, None)),
        check_vma=False,
    )
```

```python
import functools

import jax
import jax.numpy as jnp
from jax import lax
from jax.experimental import pallas as pl
from jax.experimental.pallas import tpu as pltpu
from jax.sharding import PartitionSpec as P

epsilon = 1e-06
HIGHEST = lax.Precision.HIGHEST
MESH = pl.DeviceIdType.MESH
f32 = jnp.float32
bf16 = jnp.bfloat16


def solve_normal(gram_mat, rhs_rows):
    factor_low = jnp.linalg.cholesky(gram_mat)
    return jax.scipy.linalg.cho_solve((factor_low, True), rhs_rows.T).T


def self_gram(rows_data):
    return jnp.dot(rows_data.T, rows_data, precision=HIGHEST, preferred_element_type=f32)


def body(tensor, factor_b, factor_c):
    rank_cols = factor_b.shape[-1]
    own_b = factor_b.reshape(-1, rank_cols)
    own_c = factor_c.reshape(-1, rank_cols)
    rows_i, rows_j, rows_k = tensor.shape
    block_c = lax.all_gather(own_c.astype(bf16), ("ia", "ja"), axis=0, tiled=True)
    partial_value = jnp.einsum("ijk,kr->irj", tensor, block_c, preferred_element_type=f32).astype(bf16)
    block_b = lax.all_gather(own_b.astype(bf16), ("ia", "ka"), axis=0, tiled=True)
    mode_local = jnp.einsum("irj,jr->ir", partial_value, block_b, preferred_element_type=f32)
    mode_a = lax.psum(mode_local, ("ja", "ka"))
    gram_b, gram_c = lax.psum((self_gram(own_b), self_gram(own_c)), ("ia", "ja", "ka"))
    a_new = solve_normal(gram_b * gram_c, mode_a)
    count_i = rows_i * lax.axis_size("ia")
    squares = lax.psum(jnp.sum(a_new * a_new, axis=0), "ia")
    factor_a = a_new * lax.rsqrt(squares / count_i + epsilon)
    gram_a = lax.psum(self_gram(factor_a), "ia")
    cast_a = factor_a.astype(bf16)
    mode_b = lax.psum_scatter(
        jnp.einsum("irj,ir->jr", partial_value, cast_a, preferred_element_type=f32),
        ("ia", "ka"),
        scatter_dimension=0,
        tiled=True,
    )
    b_new = solve_normal(gram_a * gram_c, mode_b)
    sums_b = lax.psum(jnp.sum(b_new * b_new, axis=0), ("ia", "ja", "ka"))
    count_j = rows_j * lax.axis_size("ja")
    out_rows = b_new * lax.rsqrt(sums_b / count_j + epsilon)
    return (factor_a, out_rows.reshape(factor_b.shape))


def dot0(a, b):
    return lax.dot_general(a, b, (((0,), (0,)), ((), ())), precision=HIGHEST, preferred_element_type=f32)


def sweep_inverse(mat, rank):
    lane = lax.rem(lax.broadcasted_iota(jnp.int32, mat.shape, 1), rank)
    row_id = lax.broadcasted_iota(jnp.int32, mat.shape, 0)
    diag = jnp.where(lane == row_id, mat, 0.0)
    scale = lax.rsqrt(jnp.sum(diag, axis=0, keepdims=True))
    scale = lax.rsqrt(jnp.sum(diag[:, :rank], axis=1, keepdims=True)) * scale
    mat = mat * scale
    for k in range(0, rank, 2):
        col1 = jnp.broadcast_to(mat[:, k : k + 1], mat.shape)
        col2 = jnp.broadcast_to(mat[:, k + 1 : k + 2], mat.shape)
        row1, row2 = mat[k : k + 1, :], mat[k + 1 : k + 2, :]
        p11, p12, p22 = col1[k : k + 1, :], col2[k : k + 1, :], col2[k + 1 : k + 2, :]
        inv = 1.0 / (p11 * p22 - p12 * p12)
        q11, q12, q22 = p22 * inv, -p12 * inv, p11 * inv
        new1 = q11 * row1 + q12 * row2
        new2 = q12 * row1 + q22 * row2
        new = mat - col1 * new1 - col2 * new2
        new = jnp.where(lane == k, q11 * col1 + q12 * col2, new)
        new = jnp.where(lane == k + 1, q12 * col1 + q22 * col2, new)
        lane1 = lane[0:1, :]
        new1 = jnp.where(lane1 == k, -q11, jnp.where(lane1 == k + 1, -q12, new1))
        new2 = jnp.where(lane1 == k, -q12, jnp.where(lane1 == k + 1, -q22, new2))
        mat = jnp.where(row_id == k, new1, jnp.where(row_id == k + 1, new2, new))
    return -mat * scale


def kernel(
    dims, x_hbm, b_ref, c_ref, fa_out, fb_out,
    xv, yv, bhi, blo, cbuf, bq, gbs, gcs, mas, mabuf, fas, mbs, mbr, sbuf,
    x_sem, send, recv,
):
    ni, nj, nk = dims
    pi, pj, pk = lax.axis_index("ia"), lax.axis_index("ja"), lax.axis_index("ka")
    n_b, n_c, n_all = ni * nk, ni * nj, ni * nj * nk
    slot_b, slot_c = pi * nk + pk, pi * nj + pj
    me = (pi * nj + pj) * nk + pk
    rows_i, rows_j, _ = xv.shape
    rank = b_ref.shape[-1]
    half = b_ref.shape[0] // 2
    rows_c = c_ref.shape[0]

    def dev_b(t):
        return (t // nk, pj, lax.rem(t, nk))

    def dev_c(t):
        return (t // nj, lax.rem(t, nj), pk)

    def dev_all(t):
        return (t // (nj * nk), lax.rem(t // nk, nj), lax.rem(t, nk))

    def copy_to(src, dst, s, dev):
        return pltpu.make_async_remote_copy(
            src_ref=src, dst_ref=dst, send_sem=send.at[s], recv_sem=recv.at[s], device_id=dev, device_id_type=MESH
        )

    def spread(buf, s, mine, n, dev):
        def step(d, carry):
            copy_to(buf.at[mine], buf.at[mine], s, dev(lax.rem(mine + d, n))).start()
            return carry

        lax.fori_loop(1, n, step, 0)

    def all_of(buf, s, n, dev):
        rest = buf.at[pl.ds(0, n - 1)]
        return copy_to(rest, rest, s, dev(0))

    load_x = pltpu.make_async_copy(x_hbm, xv, x_sem)
    load_x.start()

    barrier = pltpu.get_barrier_semaphore()

    def greet(d, carry):
        pl.semaphore_signal(barrier, inc=1, device_id=dev_all(lax.rem(me + d, n_all)), device_id_type=MESH)
        return carry

    lax.fori_loop(1, n_all, greet, 0)

    own_b = b_ref[...]
    own_c = c_ref[...]
    wide_b = jnp.concatenate([own_b[:half], own_b[half:]], axis=1)
    high_b = wide_b.astype(bf16)
    bhi[slot_b] = high_b
    blo[slot_b] = (wide_b - high_b.astype(f32)).astype(bf16)
    cbuf[slot_c] = jnp.concatenate([own_c[: rows_c // 2], own_c[rows_c // 2 :]], axis=1)

    pl.semaphore_wait(barrier, n_all - 1)

    spread(cbuf, 0, slot_c, n_c, dev_c)
    spread(bhi, 1, slot_b, n_b, dev_b)

    all_of(cbuf, 0, n_c, dev_c).wait_recv()
    c_all = cbuf[...]
    first = lax.broadcasted_iota(jnp.int32, c_all.shape, 2) < rank
    zero = jnp.zeros_like(c_all)
    c_odd = jnp.where(first, zero, c_all).reshape(n_c * rows_c // 2, 2 * rank)
    c_odd = pltpu.roll(c_odd, rank, 1).reshape(c_all.shape)
    c_left = jnp.concatenate([jnp.where(first, c_all, zero), c_odd], axis=1).reshape(n_c * rows_c, 2 * rank)
    c_right = pltpu.roll(c_left, rank, 1)
    c_two = jnp.concatenate([c_left, c_right], axis=0).astype(bf16)
    c_all = c_left + c_right
    gcs[pk] = dot0(c_all, c_all)[:rank]

    def send_gc(d, carry):
        copy_to(gcs.at[pk], gcs.at[pk], 2, (pi, pj, lax.rem(pk + d, nk))).start()
        return carry

    lax.fori_loop(1, nk, send_gc, 0)
    spread(blo, 7, slot_b, n_b, dev_b)
    load_x.wait()

    def make_y(i, carry):
        x = xv[i].reshape(n_b, 2 * half, xv.shape[2])
        left = x[:, :half].reshape(n_b * half, xv.shape[2])
        right = x[:, half:].reshape(n_b * half, xv.shape[2])
        y = jnp.dot(jnp.concatenate([left, right], axis=1), c_two, preferred_element_type=f32)
        yv[i] = y.astype(bf16)
        return carry

    lax.fori_loop(0, rows_i, make_y, 0)

    all_of(bhi, 1, n_b, dev_b).wait_recv()
    bq[...] = bhi[...].reshape(n_b * half, 2 * rank).astype(f32)

    def make_ma(i, carry):
        mas[pl.ds(i, 1), :] = jnp.sum(yv[i].astype(f32) * bq[...], axis=0, keepdims=True)
        return carry

    lax.fori_loop(0, rows_i, make_ma, 0)
    part = mas[...] + pltpu.roll(mas[...], rank, 1)
    low = lax.broadcasted_iota(jnp.int32, (rows_i // 2, 2 * rank), 1) < rank
    mabuf[me] = jnp.where(low, part[: rows_i // 2], part[rows_i // 2 :])
    spread(mabuf, 4, me, n_all, dev_all)

    all_of(blo, 7, n_b, dev_b).wait_recv()
    b_all = bq[...] + blo[...].reshape(n_b * half, 2 * rank).astype(f32)
    gram = dot0(b_all, b_all)
    low = lax.broadcasted_iota(jnp.int32, (rank, 2 * rank), 1) < rank
    gram = jnp.where(low, gram[:rank], gram[rank:])
    gbs[pj] = gram + pltpu.roll(gram, rank, 1)

    def send_gb(d, carry):
        copy_to(gbs.at[pj], gbs.at[pj], 3, (pi, lax.rem(pj + d, nj), pk)).start()
        return carry

    lax.fori_loop(1, nj, send_gb, 0)

    all_of(gcs, 2, nk, dev_b).wait_recv()
    all_of(gbs, 3, nj, dev_b).wait_recv()
    gram_c = jnp.sum(gcs[...], axis=0)
    inv_a = sweep_inverse(jnp.sum(gbs[...], axis=0) * gram_c, rank)

    all_of(mabuf, 4, n_all, dev_all).wait_recv()
    mode_a = jnp.sum(mabuf[...].reshape(ni, nj * nk, rows_i // 2, 2 * rank), axis=1)
    first = lax.broadcasted_iota(jnp.int32, mode_a.shape, 2) < rank
    zero = jnp.zeros_like(mode_a)
    mode_a = jnp.concatenate([jnp.where(first, mode_a, zero), jnp.where(first, zero, mode_a)], axis=1)
    mode_a = mode_a.reshape(ni * rows_i, 2 * rank)
    a_new = jnp.dot(
        mode_a, jnp.concatenate([inv_a, inv_a], axis=0), precision=HIGHEST, preferred_element_type=f32
    )
    squares = jnp.sum(a_new * a_new, axis=0, keepdims=True)
    factor_a = a_new * lax.rsqrt(squares / (ni * rows_i) + epsilon)
    fas[...] = factor_a
    own_a = fas[pl.ds(pl.multiple_of(pi * rows_i, rows_i), rows_i), :]
    fa_out[...] = own_a[:, :rank]
    cast_a = own_a.astype(bf16).astype(f32)

    def make_mb(d, carry):
        t = lax.rem(slot_b + d, n_b)
        rows = pl.ds(pl.multiple_of(t * half, half), half)
        total = yv[0, rows, :].astype(f32) * cast_a[0:1]
        for i in range(1, rows_i):
            total += yv[i, rows, :].astype(f32) * cast_a[i : i + 1]
        mbs[t] = total.astype(bf16)

        copy_to(mbs.at[t], mbr.at[slot_b], 5, dev_b(t)).start()
        return carry

    lax.fori_loop(1, n_b, make_mb, 0)
    rows = pl.ds(pl.multiple_of(slot_b * half, half), half)
    total = yv[0, rows, :].astype(f32) * cast_a[0:1]
    for i in range(1, rows_i):
        total += yv[i, rows, :].astype(f32) * cast_a[i : i + 1]
    mbr[slot_b] = total.astype(bf16)

    gram_a = dot0(factor_a, factor_a)[:rank]
    inv_b = sweep_inverse(gram_a * gram_c, rank)
    zero = jnp.zeros_like(inv_b)
    inv_two = jnp.concatenate([jnp.where(low, inv_b, zero), jnp.where(low, zero, inv_b)], axis=0)

    all_of(mbr, 5, n_b, dev_b).wait_recv()
    mode_b = jnp.sum(mbr[...].astype(f32), axis=0)
    b_new = jnp.dot(mode_b, inv_two, precision=HIGHEST, preferred_element_type=f32)
    sbuf[me] = jnp.sum(b_new * b_new, axis=0, keepdims=True)
    spread(sbuf, 6, me, n_all, dev_all)

    all_of(cbuf, 0, n_c, dev_c).wait_send()
    all_of(bhi, 1, n_b, dev_b).wait_send()
    all_of(blo, 7, n_b, dev_b).wait_send()
    all_of(gcs, 2, nk, dev_b).wait_send()
    all_of(gbs, 3, nj, dev_b).wait_send()
    all_of(mabuf, 4, n_all, dev_all).wait_send()
    all_of(mbr, 5, n_b, dev_b).wait_send()

    all_of(sbuf, 6, n_all, dev_all).wait_recv()
    sums = jnp.broadcast_to(jnp.sum(sbuf[...], axis=0), (8, 2 * rank))
    sums = (sums + pltpu.roll(sums, rank, 1))[0:1]
    out = b_new * lax.rsqrt(sums / (nj * rows_j) + epsilon)
    fb_out[0:half, :] = out[:, :rank]
    fb_out[half:, :] = out[:, rank:]
    all_of(sbuf, 6, n_all, dev_all).wait_send()


def place(a_ref, b_ref, a_out, b_out, sem):
    first = pltpu.make_async_copy(a_ref, a_out, sem.at[0])
    second = pltpu.make_async_copy(b_ref, b_out, sem.at[1])
    second.start()
    first.start()
    second.wait()
    first.wait()


def fused(dims, tensor, factor_b, factor_c):
    ni, nj, nk = dims
    rank = factor_b.shape[-1]
    own_b = factor_b.reshape(-1, rank)
    own_c = factor_c.reshape(-1, rank)
    rows_i, rows_j, rows_k = tensor.shape
    half = own_b.shape[0] // 2
    n_b, n_c, n_all = ni * nk, ni * nj, ni * nj * nk
    wide = 2 * rank
    vmem = pl.BlockSpec(memory_space=pltpu.VMEM)
    fa, fb = pl.pallas_call(
        functools.partial(kernel, dims),
        out_shape=(
            jax.ShapeDtypeStruct((rows_i, rank), f32),
            jax.ShapeDtypeStruct(own_b.shape, f32),
        ),
        in_specs=[pl.BlockSpec(memory_space=pl.ANY), vmem, vmem],
        out_specs=(vmem, vmem),
        scratch_shapes=[
            pltpu.VMEM(tensor.shape, bf16),
            pltpu.VMEM((rows_i, n_b * half, wide), bf16),
            pltpu.VMEM((n_b, half, wide), bf16),
            pltpu.VMEM((n_b, half, wide), bf16),
            pltpu.VMEM((n_c, own_c.shape[0] // 2, wide), f32),
            pltpu.VMEM((n_b * half, wide), f32),
            pltpu.VMEM((nj, rank, wide), f32),
            pltpu.VMEM((nk, rank, wide), f32),
            pltpu.VMEM((rows_i, wide), f32),
            pltpu.VMEM((n_all, rows_i // 2, wide), f32),
            pltpu.VMEM((ni * rows_i, wide), f32),
            pltpu.VMEM((n_b, half, wide), bf16),
            pltpu.VMEM((n_b, half, wide), bf16),
            pltpu.VMEM((n_all, 1, wide), f32),
            pltpu.SemaphoreType.DMA,
            pltpu.SemaphoreType.DMA((8,)),
            pltpu.SemaphoreType.DMA((8,)),
        ],
        compiler_params=pltpu.CompilerParams(
            collective_id=0, has_side_effects=True, vmem_limit_bytes=63 * 1024 * 1024
        ),
    )(tensor, own_b, own_c)
    fa, fb = pl.pallas_call(
        place,
        out_shape=(jax.ShapeDtypeStruct(fa.shape, f32), jax.ShapeDtypeStruct(fb.shape, f32)),
        in_specs=[vmem, vmem],
        out_specs=(pl.BlockSpec(memory_space=pl.ANY), pl.BlockSpec(memory_space=pl.ANY)),
        scratch_shapes=[pltpu.SemaphoreType.DMA((2,))],
    )(fa, fb)
    return fa, fb.reshape(factor_b.shape)


def solution(mesh):
    dims = tuple(mesh.shape[a] for a in ("ia", "ja", "ka"))

    def step(tensor, factor_b, factor_c):
        whole_tiles = (
            factor_b.shape[-2] % 32 == 0
            and factor_c.shape[-2] % 8 == 0
            and tensor.shape[0] % 8 == 0
            and factor_b.shape[-1] == 64
        )
        if whole_tiles:
            return fused(dims, tensor, factor_b, factor_c)
        return body(tensor, factor_b, factor_c)

    return jax.shard_map(
        step,
        mesh=mesh,
        in_specs=(
            P("ia", "ja", "ka"),
            P("ia", "ja", "ka", None, None),
            P("ka", "ia", "ja", None, None),
        ),
        out_specs=(P("ia", None), P("ia", "ja", "ka", None, None)),
        check_vma=False,
    )
```
